32 devices in a mesh: wide: 8 (over z, core), narrow: 4 (over y, x).
Axes of the slice: x: 2, y: 2, z: 4, core: 2. Of those that a mesh axis runs over, the one named last changes fastest.
Arguments:
- block_states: bfloat16 [16, 64, 4096], P('wide', None, 'narrow'), may hold values from -6 to 6
- attn_gain: float32 [4096], replicated, may hold values from 0.1 to 1.9
- ffn_gain: float32 [4096], replicated, may hold values from 0.1 to 1.9
- final_gain: float32 [4096], replicated, may hold values from 0.1 to 1.9
- w_query: bfloat16 [4096, 4096], P(None, 'narrow'), may hold values from -0.09375 to 0.09375
- w_keyval: bfloat16 [4096, 1024], replicated, may hold values from -0.09375 to 0.09375
- w_out: bfloat16 [4096, 4096], P('narrow'), may hold values from -0.09375 to 0.09375
- w_gate: bfloat16 [4096, 1024], P(None, 'narrow'), may hold values from -0.09375 to 0.09375
- w_up: bfloat16 [4096, 1024], P(None, 'narrow'), may hold values from -0.09375 to 0.09375
- w_down: bfloat16 [1024, 4096], P('narrow'), may hold values from -0.1875 to 0.1875
- w_head: bfloat16 [4096, 32768], P(None, ('wide', 'narrow')), may hold values from -8 to 8
- cache: bfloat16 [16, 512, 4, 256], P('wide'), may hold values from -2000 to 2000
- prefix_lengths: int32 [16], P('wide'), may hold values from 128 to 512, as said below
- masked_positions: int32 [8, 64], replicated, may hold values from 0 to 63, as said below
Outputs:
- log_probs: float32 [512, 32768], P(None, ('wide', 'narrow'))
- confidence: float32 [8, 64], replicated
The draws below stay inside these ranges and needn't reach their ends.
Inputs may be any that keep to these rules, and one draw needn't show every extreme that they name: `prefix_lengths`: some request branch has exactly 512 valid positions. `masked_positions`: the 64 positions of one request are distinct.
All inputs are finite; a program needn't handle non-finite values.
Results may differ from the reference program's by a relative error of at most 0.024.
The reference program's roundings to bfloat16 on the way count: a program that leaves them out, or rounds other values in their place, can miss the bound.
Values may be sent and summed in bfloat16 or wider, within the bound.
A program may use at most 128 MiB of HBM per device.

```python
import math
import jax
import jax.numpy as jnp
from jax import lax

D = 4096
HEADS = 32
KVH = 4
HD = 128
SH = 1024
BLOCK = 64
PREFIX = 512
MASKED = 64
REQ = 8
V = 32768


def draw_w_head(key, part):
    key_base, key_scale = jax.random.split(jax.random.fold_in(key, 11), 2)
    base = jax.random.truncated_normal(key_base, -6.0, 6.0, (D, V), jnp.float32) * D ** (-0.5)
    col_scale = jnp.exp(jax.random.uniform(key_scale, (V,), jnp.float32, 0.0, jnp.log(10.0)))
    return jnp.clip(base * col_scale[None, :], -8.0, 8.0).astype(jnp.bfloat16)


def draw_cache(key, part):
    key_base = jax.random.fold_in(jax.random.fold_in(key, 23), 0)
    base = jax.random.truncated_normal(key_base, -6.0, 6.0, (2 * REQ, PREFIX, KVH, 2 * HD), jnp.float32)
    return base.astype(jnp.bfloat16)


def draw_prefix_lengths(key, part):
    key_len, key_which = jax.random.split(jax.random.fold_in(key, 37))
    lengths = jax.random.randint(key_len, (2 * REQ,), PREFIX // 4, PREFIX + 1)
    which = jax.random.randint(key_which, (), 0, 2 * REQ)
    return jnp.where(jnp.arange(2 * REQ) == which, PREFIX, lengths).astype(jnp.int32)


def draw_masked_positions(key, part):
    keys = jax.random.split(jax.random.fold_in(key, 41), REQ)
    chosen = jax.vmap(lambda single: jax.random.permutation(single, BLOCK)[:MASKED])(keys)
    return chosen.astype(jnp.int32)


def levels(own_key, shape, cuts, low, high):
    def one(position, shards_of):
        heights = jax.random.uniform(jax.random.fold_in(jax.random.fold_in(own_key, 6), position), (shards_of,), jnp.float32, low / len(cuts), high / len(cuts))
        return jnp.repeat(jnp.exp(heights), shape[position] // shards_of).reshape((-1,) + (1,) * (len(shape) - position - 1))

    factor_of = one(*cuts[0])
    for cut in cuts[1:]:
        factor_of = factor_of * one(*cut)
    return factor_of


def bell_draw(stream_key, extent, spread, reach, pieces=(), held_as=jnp.bfloat16):
    values = jax.random.normal(stream_key, extent, jnp.float32) * spread
    if len(pieces) > 0:
        values = levels(stream_key, extent, pieces, -0.22, 0.18) * values
    return jnp.clip(values, min=-reach, max=reach).astype(held_as)


def setup_inputs(seed: int = 0) -> dict:
    seeds = jax.random.split(jax.random.key(seed), 15)
    return {
        "block_states": bell_draw(seeds[0], (2 * REQ, BLOCK, D), 1.0, 6.0, ((0, 8), (2, 4))),
        "attn_gain": jnp.clip(1.0 + 0.18 * jax.random.normal(seeds[1], (D,), jnp.float32), 0.1, 1.9),
        "ffn_gain": jnp.clip(1.0 + 0.18 * jax.random.normal(seeds[2], (D,), jnp.float32), 0.1, 1.9),
        "final_gain": jnp.clip(1.0 + 0.18 * jax.random.normal(seeds[3], (D,), jnp.float32), 0.1, 1.9),
        "w_query": bell_draw(seeds[4], (D, HEADS * HD), D ** -0.5, 0.09375, ((1, 4),)),
        "w_keyval": bell_draw(seeds[5], (D, 2 * KVH * HD), D ** -0.5, 0.09375),
        "w_out": bell_draw(seeds[6], (HEADS * HD, D), (HEADS * HD) ** -0.5, 0.09375, ((0, 4),)),
        "w_gate": bell_draw(seeds[7], (D, SH), D ** -0.5, 0.09375, ((1, 4),)),
        "w_up": bell_draw(seeds[8], (D, SH), D ** -0.5, 0.09375, ((1, 4),)),
        "w_down": bell_draw(seeds[9], (SH, D), SH ** -0.5, 0.1875, ((0, 4),)),
        "w_head": draw_w_head(jax.random.fold_in(seeds[14], 71), 0),
        "cache": draw_cache(jax.random.fold_in(seeds[14], 71), 0),
        "prefix_lengths": draw_prefix_lengths(jax.random.fold_in(seeds[14], 71), 0),
        "masked_positions": draw_masked_positions(jax.random.fold_in(seeds[14], 71), 0),
    }


EPS = 1e-06
GUIDE = 1.5

def rms_scale(rows, gain):
    return rows * lax.rsqrt(lax.optimization_barrier(jnp.mean(rows * rows, axis=-1, keepdims=True)) + EPS) * gain

def attend_one(operands):
    query, cache_one, block_kv, length = operands
    group = HEADS // KVH
    query_four = query.astype(jnp.float32).reshape(MASKED, KVH, group, HD)
    scale = 1.0 / math.sqrt(HD)
    pre_keys = cache_one[:, :, :HD].astype(jnp.float32)
    pre_vals = cache_one[:, :, HD:].astype(jnp.float32)
    blk_keys = block_kv[:, :, 0, :].astype(jnp.float32)
    blk_vals = block_kv[:, :, 1, :].astype(jnp.float32)
    pre_scores = jnp.einsum('mkgd,pkd->kgmp', query_four, pre_keys) * scale
    live = jnp.arange(PREFIX) < length
    pre_scores = jnp.where(live, pre_scores, -jnp.inf)
    blk_scores = jnp.einsum('mkgd,pkd->kgmp', query_four, blk_keys) * scale
    scores = jnp.concatenate([pre_scores, blk_scores], axis=-1)
    peak = lax.optimization_barrier(jnp.max(scores, axis=-1, keepdims=True))
    weights = jnp.exp(scores - peak)
    probs = (weights / lax.optimization_barrier(jnp.sum(weights, axis=-1, keepdims=True))).astype(jnp.bfloat16)
    values = jnp.concatenate([pre_vals, blk_vals], axis=0)
    out = jnp.einsum('kgmp,pkd->mkgd', probs.astype(jnp.float32), values)
    return out.reshape(MASKED, HEADS * HD).astype(jnp.bfloat16)

def reference(block_states, attn_gain, ffn_gain, final_gain, w_query, w_keyval, w_out, w_gate, w_up, w_down, w_head, cache, prefix_lengths, masked_positions):
    states = block_states.astype(jnp.float32)
    normed = rms_scale(states, attn_gain).astype(jnp.bfloat16)
    keyval = jnp.einsum('bld,dc->blc', normed.astype(jnp.float32), w_keyval.astype(jnp.float32)).astype(jnp.bfloat16)
    keyval = keyval.reshape(2 * REQ, BLOCK, KVH, 2, HD)
    both_pos = jnp.concatenate([masked_positions, masked_positions], axis=0)
    picked = jax.vmap(lambda rows, idx: rows[idx])(block_states, both_pos)
    picked_normed = jax.vmap(lambda rows, idx: rows[idx])(normed, both_pos)
    query = jnp.einsum('bmd,dc->bmc', picked_normed.astype(jnp.float32), w_query.astype(jnp.float32)).astype(jnp.bfloat16)
    attended = lax.map(attend_one, (query, cache, keyval, prefix_lengths))
    first = picked.astype(jnp.float32) + jnp.einsum('bmc,cd->bmd', attended.astype(jnp.float32), w_out.astype(jnp.float32))
    ffn_in = rms_scale(first, ffn_gain).astype(jnp.bfloat16).astype(jnp.float32)
    gate_act = jnp.einsum('bmd,dc->bmc', ffn_in, w_gate.astype(jnp.float32))
    up_act = jnp.einsum('bmd,dc->bmc', ffn_in, w_up.astype(jnp.float32))
    hidden = (jax.nn.silu(gate_act) * up_act).astype(jnp.bfloat16)
    second = first + jnp.einsum('bmc,cd->bmd', hidden.astype(jnp.float32), w_down.astype(jnp.float32))
    final = rms_scale(second, final_gain)
    cond_rows = final[:REQ]
    uncond_rows = final[REQ:]
    guided = (uncond_rows + GUIDE * (cond_rows - uncond_rows)).astype(jnp.bfloat16).reshape(REQ * MASKED, D)
    logits = jnp.dot(guided, w_head, preferred_element_type=jnp.float32)
    peak = lax.optimization_barrier(jnp.max(logits, axis=-1))
    total = lax.optimization_barrier(jnp.sum(jnp.exp(logits - peak[:, None]), axis=-1))
    lse = peak + jnp.log(total)
    log_probs = logits - lse[:, None]
    confidence = jnp.exp(peak - lse).reshape(REQ, MASKED)
    return (log_probs, confidence)
```

```python
import functools
import math

import jax
import jax.numpy as jnp
from jax import lax
from jax.experimental import pallas as pl
from jax.experimental.pallas import tpu as pltpu
from jax.sharding import PartitionSpec as P

KVH = 4
HD = 128
EPS = 1e-06
GUIDE = 1.5
CHUNKS = 4
MESH = pl.DeviceIdType.MESH
F32 = jnp.float32
BF16 = jnp.bfloat16


def dot(a, b):
    return jnp.dot(a, b, preferred_element_type=F32)


def push(src, dst, send, recv, where):
    return pltpu.make_async_remote_copy(
        src_ref=src, dst_ref=dst, send_sem=send, recv_sem=recv, device_id=where, device_id_type=MESH
    )


def greet(others):
    barrier = pltpu.get_barrier_semaphore()
    for where in others:
        pl.semaphore_signal(barrier, inc=1, device_id=where, device_id_type=MESH)
    pl.semaphore_wait(barrier, len(others))


def gather_kernel(n_narrow, mine, gain, full_out, normed_out, full, send, recv, local):
    n = lax.axis_index("narrow")
    w = lax.axis_index("wide")
    cols = mine.shape[1]
    others = [{"wide": w, "narrow": lax.rem(n + d, n_narrow)} for d in range(1, n_narrow)]
    span = pl.ds(pl.multiple_of(n * cols, cols), cols)
    keep = pltpu.make_async_copy(mine, full.at[:, span], local)
    keep.start()
    greet(others)
    copies = [
        push(mine, full.at[:, span], send.at[d], recv.at[d], where) for d, where in enumerate(others)
    ]
    for copy in copies:
        copy.start()
    keep.wait()
    for copy in copies:
        copy.wait()

    rows = full.shape[0]
    step = 16

    def norm_rows(i, carry):
        at = pl.ds(pl.multiple_of(i * step, step), step)
        raw = full[at, :]
        value = raw.astype(F32)
        full_out[at, :] = raw
        scale = lax.rsqrt(jnp.mean(value * value, axis=-1, keepdims=True) + EPS)
        normed_out[at, :] = (value * scale * gain[...]).astype(BF16)
        return carry

    lax.fori_loop(0, rows // step, norm_rows, 0)


def gather_rows(n_narrow, mine, gain):
    rows, cols = mine.shape
    shape = jax.ShapeDtypeStruct((rows, cols * n_narrow), BF16)
    vmem = pl.BlockSpec(memory_space=pltpu.VMEM)
    return pl.pallas_call(
        functools.partial(gather_kernel, n_narrow),
        out_shape=(shape, shape),
        in_specs=[vmem, vmem],
        out_specs=(vmem, vmem),
        scratch_shapes=[
            pltpu.VMEM(shape.shape, BF16),
            pltpu.SemaphoreType.DMA((n_narrow - 1,)),
            pltpu.SemaphoreType.DMA((n_narrow - 1,)),
            pltpu.SemaphoreType.DMA,
        ],
        compiler_params=pltpu.CompilerParams(
            collective_id=0, has_side_effects=True, vmem_limit_bytes=24 * 2**20
        ),
    )(mine, gain)


def tail_kernel(
    n_wide,
    n_narrow,
    attended,
    picked,
    ffn_gain,
    final_gain,
    w_out,
    w_gate,
    w_up,
    w_down,
    w_head,
    logits,
    stats,
    wo,
    wg,
    wu,
    wd,
    wh,
    part,
    sent_a,
    sent_b,
    got_a,
    got_b,
    first,
    ffn_in,
    gate_acc,
    up_acc,
    swap_out,
    swap_in,
    guided,
    row_peak,
    row_total,
    board,
    load_sem,
    rs_send,
    rs_recv,
    ag_send,
    ag_recv,
    rt_send,
    rt_recv,
    swap_sem,
    z_send,
    z_recv,
    n_send,
    n_recv,
    s_send,
    s_recv,
    st_send,
    st_recv,
):
    n = lax.axis_index("narrow")
    w = lax.axis_index("wide")
    half = n_wide // 2
    pairs = n_wide // 2
    rows, width = ffn_in.shape
    mine = rows // n_narrow
    chunk = width // CHUNKS
    near = [lax.rem(n + d, n_narrow) for d in range(n_narrow)]
    far = [lax.rem(w + 2 * k, n_wide) for k in range(pairs)]
    twin = w + 1 - 2 * lax.rem(w, 2)
    near_at = [{"wide": w, "narrow": i} for i in near]
    far_at = [{"wide": i, "narrow": n} for i in far]
    twin_at = {"wide": twin, "narrow": n}

    def cols(c):
        return pl.ds(pl.multiple_of(c * chunk, chunk), chunk)

    def block_rows(i):
        return pl.ds(pl.multiple_of(i * mine, mine), mine)

    own = block_rows(n)
    loads = [
        pltpu.make_async_copy(w_out.at[:, cols(c)], wo.at[:, cols(c)], load_sem.at[c])
        for c in range(CHUNKS)
    ]
    for i, (src, dst) in enumerate(((w_gate, wg), (w_up, wu), (w_down, wd), (w_head, wh))):
        loads.append(pltpu.make_async_copy(src, dst, load_sem.at[CHUNKS + i]))
    for load in loads:
        load.start()
    greet(near_at[1:] + far_at[1:] + [twin_at])

    def scatter(sent, got, send, recv, c):
        return [
            push(
                sent.at[block_rows(near[d]), cols(c)],
                got.at[d - 1, :, cols(c)],
                send.at[c, d - 1],
                recv.at[c, d - 1],
                near_at[d],
            )
            for d in range(1, n_narrow)
        ]

    for c in range(CHUNKS):
        loads[c].wait()
        value = dot(attended[...], wo[:, cols(c)])
        part[:, cols(c)] = value
        sent_a[:, cols(c)] = value.astype(BF16)
        for copy in scatter(sent_a, got_a, rs_send, rs_recv, c):
            copy.start()
    square = jnp.zeros((mine, 1), F32)
    for c in range(CHUNKS):
        for copy in scatter(sent_a, got_a, rs_send, rs_recv, c):
            copy.wait_recv()
        value = picked[:, cols(c)].astype(F32) + part[own, cols(c)]
        for d in range(n_narrow - 1):
            value = value + got_a[d, :, cols(c)].astype(F32)
        first[:, cols(c)] = value
        square = square + jnp.sum(value * value, axis=-1, keepdims=True)
    scale = lax.rsqrt(square / width + EPS)

    def spread(c):
        return [
            push(
                ffn_in.at[own, cols(c)],
                ffn_in.at[own, cols(c)],
                ag_send.at[c, d - 1],
                ag_recv.at[c, d - 1],
                near_at[d],
            )
            for d in range(1, n_narrow)
        ]

    for c in range(CHUNKS):
        ffn_in[own, cols(c)] = (first[:, cols(c)] * scale * ffn_gain[:, cols(c)]).astype(BF16)
        for copy in spread(c):
            copy.start()
    for load in loads[CHUNKS : CHUNKS + 3]:
        load.wait()
    for c in range(CHUNKS):
        for copy in spread(c):
            copy.wait_recv()
        gate_part = dot(ffn_in[:, cols(c)], wg[cols(c), :])
        up_part = dot(ffn_in[:, cols(c)], wu[cols(c), :])
        if c == 0:
            gate_acc[...] = gate_part
            up_acc[...] = up_part
        else:
            gate_acc[...] += gate_part
            up_acc[...] += up_part
    gate = gate_acc[...]
    hidden = (gate / (1.0 + jnp.exp(-gate)) * up_acc[...]).astype(BF16)

    for c in range(CHUNKS):
        value = dot(hidden, wd[:, cols(c)])
        part[:, cols(c)] = value
        sent_b[:, cols(c)] = value.astype(BF16)
        for copy in scatter(sent_b, got_b, rt_send, rt_recv, c):
            copy.start()
    square = jnp.zeros((mine, 1), F32)
    for c in range(CHUNKS):
        for copy in scatter(sent_b, got_b, rt_send, rt_recv, c):
            copy.wait_recv()
        value = first[:, cols(c)] + part[own, cols(c)]
        for d in range(n_narrow - 1):
            value = value + got_b[d, :, cols(c)].astype(F32)
        first[:, cols(c)] = value
        square = square + jnp.sum(value * value, axis=-1, keepdims=True)
    scale = lax.rsqrt(square / width + EPS)
    first[...] = first[...] * scale * final_gain[...]

    upper = w // half
    wide_half = width // 2

    def side(i):
        return pl.ds(pl.multiple_of(i * wide_half, wide_half), wide_half)

    swap_out[...] = first[:, side(1 - upper)].astype(BF16)
    swap = push(
        swap_out,
        swap_in,
        swap_sem.at[0],
        swap_sem.at[1],
        {"wide": lax.rem(w + half, n_wide), "narrow": n},
    )
    swap.start()

    def region(source, narrow):
        start = lax.rem(source, half) * rows + narrow * mine
        return guided.at[pl.ds(pl.multiple_of(start, mine), mine), side(source // half)]

    swap.wait()
    kept = first[:, side(upper)]
    other = swap_in[...].astype(F32)
    cond = jnp.where(upper == 1, other, kept)
    uncond = jnp.where(upper == 1, kept, other)
    region(w, n)[...] = (uncond + GUIDE * (cond - uncond)).astype(BF16)

    def from_far(k):
        return lax.rem(w + n_wide - 2 * k, n_wide)

    def from_near(d):
        return lax.rem(n + n_narrow - d, n_narrow)

    def z_copy(k):
        spot = region(w, n)
        return push(spot, spot, z_send.at[k], z_recv.at[k], far_at[k])

    def n_copy(k, d):
        spot = region(from_far(k), n)
        return push(spot, spot, n_send.at[k, d], n_recv.at[k, d], near_at[d])

    def s_copy(k, d):
        spot = region(from_far(k), from_near(d))
        return push(spot, spot, s_send.at[k, d], s_recv.at[k, d], twin_at)

    for k in range(1, pairs):
        z_copy(k).start()
    for k in range(pairs):
        if k:
            z_copy(k).wait_recv()
        for d in range(1, n_narrow):
            n_copy(k, d).start()
        s_copy(k, 0).start()
    for k in range(pairs):
        for d in range(1, n_narrow):
            n_copy(k, d).wait_recv()
            s_copy(k, d).start()
    for k in range(pairs):
        for d in range(n_narrow):
            s_copy(k, d).wait_recv()

    loads[CHUNKS + 3].wait()
    tile = 256

    def logit_tile(j, carry):
        at = pl.ds(pl.multiple_of(j * tile, tile), tile)
        logits[:, at] = dot(guided[...], wh[:, at])
        return carry

    lax.fori_loop(0, logits.shape[1] // tile, logit_tile, 0)
    step = 64

    def row_stats(i, carry):
        at = pl.ds(pl.multiple_of(i * step, step), step)
        value = logits[at, :]
        top = jnp.max(value, axis=-1, keepdims=True)
        total = jnp.sum(jnp.exp(value - top), axis=-1, keepdims=True)
        row_peak[at, :] = jnp.broadcast_to(top, (step, row_peak.shape[1]))
        row_total[at, :] = jnp.broadcast_to(total, (step, row_peak.shape[1]))
        return carry

    count = logits.shape[0]
    lax.fori_loop(0, count // step, row_stats, 0)
    peak = row_peak[...].T[0:1, :]
    total = row_total[...].T[0:1, :]

    slot = 0
    for stage, places in enumerate(([twin_at], near_at[1:], far_at[1:])):
        board[slot, :, 0:count] = peak
        board[slot, :, count:] = total
        copies = [
            push(
                board.at[slot],
                board.at[slot + 1 + i],
                st_send.at[slot + 1 + i],
                st_recv.at[slot + 1 + i],
                where,
            )
            for i, where in enumerate(places)
        ]
        for copy in copies:
            copy.start()
        for copy in copies:
            copy.wait()
        top = peak
        for i in range(len(places)):
            top = jnp.maximum(top, board[slot + 1 + i, :, 0:count])
        total = total * jnp.exp(peak - top)
        for i in range(len(places)):
            got = board[slot + 1 + i]
            total = total + got[:, count:] * jnp.exp(got[:, 0:count] - top)
        peak = top
        slot += 1 + len(places)
    stats[0:1, :] = peak + jnp.log(total)
    stats[1:2, :] = 1.0 / total

    for c in range(CHUNKS):
        for copy in scatter(sent_a, got_a, rs_send, rs_recv, c):
            copy.wait_send()
        for copy in scatter(sent_b, got_b, rt_send, rt_recv, c):
            copy.wait_send()
        for copy in spread(c):
            copy.wait_send()
    for k in range(pairs):
        if k:
            z_copy(k).wait_send()
        for d in range(n_narrow):
            if d:
                n_copy(k, d).wait_send()
            s_copy(k, d).wait_send()


def tail(n_wide, n_narrow, attended, picked, ffn_gain, final_gain, *weights):
    w_out, w_gate, w_up, w_down, w_head = weights
    rows = attended.shape[0]
    width = picked.shape[1]
    mine = rows // n_narrow
    pairs = n_wide // 2
    total_rows = rows * pairs
    vocab_cols = w_head.shape[1]
    vmem = pl.BlockSpec(memory_space=pltpu.VMEM)
    hbm = pl.BlockSpec(memory_space=pl.ANY)
    near = n_narrow - 1
    slots = 3 + 1 + near + pairs - 1
    dma = pltpu.SemaphoreType.DMA
    return pl.pallas_call(
        functools.partial(tail_kernel, n_wide, n_narrow),
        out_shape=(
            jax.ShapeDtypeStruct((total_rows, vocab_cols), F32),
            jax.ShapeDtypeStruct((2, total_rows), F32),
        ),
        in_specs=[vmem] * 4 + [hbm] * 5,
        out_specs=(vmem, vmem),
        scratch_shapes=[pltpu.VMEM(v.shape, BF16) for v in weights]
        + [
            pltpu.VMEM((rows, width), F32),
            pltpu.VMEM((rows, width), BF16),
            pltpu.VMEM((rows, width), BF16),
            pltpu.VMEM((near, mine, width), BF16),
            pltpu.VMEM((near, mine, width), BF16),
            pltpu.VMEM((mine, width), F32),
            pltpu.VMEM((rows, width), BF16),
            pltpu.VMEM((rows, w_gate.shape[1]), F32),
            pltpu.VMEM((rows, w_gate.shape[1]), F32),
            pltpu.VMEM((mine, width // 2), BF16),
            pltpu.VMEM((mine, width // 2), BF16),
            pltpu.VMEM((total_rows, width), BF16),
            pltpu.VMEM((total_rows, 128), F32),
            pltpu.VMEM((total_rows, 128), F32),
            pltpu.VMEM((slots, 1, 2 * total_rows), F32),
            dma((CHUNKS + 4,)),
            dma((CHUNKS, near)),
            dma((CHUNKS, near)),
            dma((CHUNKS, near)),
            dma((CHUNKS, near)),
            dma((CHUNKS, near)),
            dma((CHUNKS, near)),
            dma((2,)),
            dma((pairs,)),
            dma((pairs,)),
            dma((pairs, n_narrow)),
            dma((pairs, n_narrow)),
            dma((pairs, n_narrow)),
            dma((pairs, n_narrow)),
            dma((slots,)),
            dma((slots,)),
        ],
        compiler_params=pltpu.CompilerParams(
            collective_id=1, has_side_effects=True, vmem_limit_bytes=60 * 2**20
        ),
    )(attended, picked, ffn_gain, final_gain, *weights)


def on_device(
    block_states,
    attn_gain,
    ffn_gain,
    final_gain,
    w_query,
    w_keyval,
    w_out,
    w_gate,
    w_up,
    w_down,
    w_head,
    cache,
    prefix_lengths,
    masked_positions,
):
    n_wide = lax.axis_size("wide")
    n_narrow = lax.axis_size("narrow")
    wide_index = lax.axis_index("wide")
    narrow_index = lax.axis_index("narrow")
    half_wide = n_wide // 2
    local_req, block, _ = block_states.shape
    masked = masked_positions.shape[1]
    width = w_query.shape[0]

    full_rows, normed = gather_rows(
        n_narrow, block_states.reshape(local_req * block, -1), attn_gain[None, :]
    )
    full_rows = full_rows.reshape(local_req, block, width)

    kv_head = narrow_index // (n_narrow // KVH)
    head_weight = lax.dynamic_slice_in_dim(w_keyval, kv_head * (2 * HD), 2 * HD, 1)
    block_kv = dot(normed, head_weight).astype(BF16).reshape(local_req, block, 2 * HD)
    cache_kv = lax.dynamic_index_in_dim(cache, kv_head, axis=2, keepdims=False)
    first_req = wide_index % half_wide * local_req
    my_positions = lax.dynamic_slice_in_dim(masked_positions, first_req, local_req, 0)
    choose = (my_positions[:, :, None] == jnp.arange(block)[None, None, :]).astype(BF16)
    picked = jnp.einsum("bml,bld->bmd", choose, full_rows, preferred_element_type=F32)
    picked = picked.astype(BF16).reshape(local_req * masked, width)
    mine = local_req * masked // n_narrow
    picked = lax.dynamic_slice_in_dim(picked, narrow_index * mine, mine, 0)
    local_heads = w_query.shape[1] // HD
    query = dot(normed, w_query).astype(BF16).reshape(local_req, block, local_heads * HD)
    query = jnp.einsum("bml,bld->bmd", choose, query, preferred_element_type=F32).astype(BF16)
    query = query.reshape(local_req, masked, local_heads, HD)
    scale = 1.0 / math.sqrt(HD)
    pre_scores = (
        jnp.einsum("bmhd,bpd->bhmp", query, cache_kv[..., :HD], preferred_element_type=F32) * scale
    )
    live = jnp.arange(cache_kv.shape[1])[None, :] < prefix_lengths[:, None]
    pre_scores = jnp.where(live[:, None, None, :], pre_scores, -jnp.inf)
    blk_scores = (
        jnp.einsum("bmhd,bld->bhml", query, block_kv[..., :HD], preferred_element_type=F32) * scale
    )
    peak = jnp.maximum(
        jnp.max(pre_scores, axis=-1, keepdims=True), jnp.max(blk_scores, axis=-1, keepdims=True)
    )
    pre_weights = jnp.exp(pre_scores - peak)
    blk_weights = jnp.exp(blk_scores - peak)
    weight_total = jnp.sum(pre_weights, axis=-1, keepdims=True) + jnp.sum(
        blk_weights, axis=-1, keepdims=True
    )
    pre_probs = (pre_weights / weight_total).astype(BF16)
    blk_probs = (blk_weights / weight_total).astype(BF16)
    attended = jnp.einsum(
        "bhmp,bpd->bmhd", pre_probs, cache_kv[..., HD:], preferred_element_type=F32
    )
    attended = attended + jnp.einsum(
        "bhml,bld->bmhd", blk_probs, block_kv[..., HD:], preferred_element_type=F32
    )
    attended = attended.astype(BF16).reshape(local_req * masked, local_heads * HD)

    logits, stats = tail(
        n_wide,
        n_narrow,
        attended,
        picked,
        ffn_gain[None, :],
        final_gain[None, :],
        w_out,
        w_gate,
        w_up,
        w_down,
        w_head,
    )
    return logits - stats[0][:, None], stats[1].reshape(-1, masked)


def solution(mesh):
    in_specs = (
        P("wide", None, "narrow"),
        P(),
        P(),
        P(),
        P(None, "narrow"),
        P(),
        P("narrow", None),
        P(None, "narrow"),
        P(None, "narrow"),
        P("narrow", None),
        P(None, ("wide", "narrow")),
        P("wide", None, None, None),
        P("wide"),
        P(),
    )
    out_specs = (P(None, ("wide", "narrow")), P())
    return jax.shard_map(
        on_device, mesh=mesh, in_specs=in_specs, out_specs=out_specs, check_vma=False
    )
```

```python
import functools
import math

import jax
import jax.numpy as jnp
from jax import lax
from jax.experimental import pallas as pl
from jax.experimental.pallas import tpu as pltpu
from jax.sharding import PartitionSpec as P

KVH = 4
HD = 128
EPS = 1e-06
GUIDE = 1.5
CHUNKS = 4
LANES = 128
MESH = pl.DeviceIdType.MESH
F32 = jnp.float32
BF16 = jnp.bfloat16


def dot(a, b):
    return jnp.dot(a, b, preferred_element_type=F32)


def push(src, dst, send, recv, where):
    return pltpu.make_async_remote_copy(
        src_ref=src, dst_ref=dst, send_sem=send, recv_sem=recv, device_id=where, device_id_type=MESH
    )


def greet(others):
    barrier = pltpu.get_barrier_semaphore()
    for where in others:
        pl.semaphore_signal(barrier, inc=1, device_id=where, device_id_type=MESH)
    pl.semaphore_wait(barrier, len(others))


def gather_kernel(n_narrow, mine, gain, full_out, normed_out, full, send, recv, local):
    n = lax.axis_index("narrow")
    w = lax.axis_index("wide")
    cols = mine.shape[1]
    others = [{"wide": w, "narrow": lax.rem(n + d, n_narrow)} for d in range(1, n_narrow)]
    span = pl.ds(pl.multiple_of(n * cols, cols), cols)
    keep = pltpu.make_async_copy(mine, full.at[:, span], local)
    keep.start()
    greet(others)
    copies = [
        push(mine, full.at[:, span], send.at[d], recv.at[d], where) for d, where in enumerate(others)
    ]
    for copy in copies:
        copy.start()
    keep.wait()
    for copy in copies:
        copy.wait()

    rows = full.shape[0]
    step = 16

    def norm_rows(i, carry):
        at = pl.ds(pl.multiple_of(i * step, step), step)
        raw = full[at, :]
        value = raw.astype(F32)
        full_out[at, :] = raw
        scale = lax.rsqrt(jnp.mean(value * value, axis=-1, keepdims=True) + EPS)
        normed_out[at, :] = (value * scale * gain[...]).astype(BF16)
        return carry

    lax.fori_loop(0, rows // step, norm_rows, 0)


def gather_rows(n_narrow, mine, gain):
    rows, cols = mine.shape
    shape = jax.ShapeDtypeStruct((rows, cols * n_narrow), BF16)
    vmem = pl.BlockSpec(memory_space=pltpu.VMEM)
    return pl.pallas_call(
        functools.partial(gather_kernel, n_narrow),
        out_shape=(shape, shape),
        in_specs=[vmem, vmem],
        out_specs=(vmem, vmem),
        scratch_shapes=[
            pltpu.VMEM(shape.shape, BF16),
            pltpu.SemaphoreType.DMA((n_narrow - 1,)),
            pltpu.SemaphoreType.DMA((n_narrow - 1,)),
            pltpu.SemaphoreType.DMA,
        ],
        compiler_params=pltpu.CompilerParams(
            collective_id=0, has_side_effects=True, vmem_limit_bytes=24 * 2**20
        ),
    )(mine, gain)


def tail_kernel(
    n_wide,
    n_narrow,
    attended,
    picked,
    ffn_gain,
    final_gain,
    w_out,
    w_gate,
    w_up,
    w_down,
    w_head,
    logits,
    stats,
    wo,
    wg,
    wu,
    wd,
    wh,
    part,
    sent_a,
    sent_b,
    got_a,
    got_b,
    first,
    ffn_in,
    gate_acc,
    up_acc,
    swap_out,
    swap_in,
    ffn_scale,
    scale_out,
    scale_in,
    guided,
    row_peak,
    row_total,
    board,
    load_sem,
    rs_send,
    rs_recv,
    ag_send,
    ag_recv,
    rt_send,
    rt_recv,
    swap_send,
    swap_recv,
    sc_send,
    sc_recv,
    l_send,
    l_recv,
    n_send,
    n_recv,
    s_send,
    s_recv,
    st_send,
    st_recv,
):
    n = lax.axis_index("narrow")
    w = lax.axis_index("wide")
    half = n_wide // 2
    pairs = n_wide // 2
    rows, width = ffn_in.shape
    mine = rows // n_narrow
    chunk = width // CHUNKS
    near = [lax.rem(n + d, n_narrow) for d in range(n_narrow)]
    far = [lax.rem(w + 2 * k, n_wide) for k in range(pairs)]
    twin = w + 1 - 2 * lax.rem(w, 2)
    near_at = [{"wide": w, "narrow": i} for i in near]
    far_at = [{"wide": i, "narrow": n} for i in far]
    twin_at = {"wide": twin, "narrow": n}
    cross_at = [{"wide": twin, "narrow": i} for i in near[1:]]
    place = w // 2
    line_at = {1: {"wide": lax.rem(w + 2, n_wide), "narrow": n}, -1: {"wide": lax.rem(w + n_wide - 2, n_wide), "narrow": n}}

    def cols(c):
        return pl.ds(pl.multiple_of(c * chunk, chunk), chunk)

    def block_rows(i):
        return pl.ds(pl.multiple_of(i * mine, mine), mine)

    own = block_rows(n)
    loads = [
        pltpu.make_async_copy(w_out.at[:, cols(c)], wo.at[:, cols(c)], load_sem.at[c])
        for c in range(CHUNKS)
    ]
    for i, (src, dst) in enumerate(((w_gate, wg), (w_up, wu), (w_down, wd), (w_head, wh))):
        loads.append(pltpu.make_async_copy(src, dst, load_sem.at[CHUNKS + i]))
    for load in loads:
        load.start()
    greet(near_at[1:] + far_at[1:] + [twin_at] + cross_at)

    def scatter(sent, got, send, recv, i, c=None):
        c = i if c is None else c
        return [
            push(
                sent.at[block_rows(near[d]), cols(c)],
                got.at[d - 1, :, cols(c)],
                send.at[i, d - 1],
                recv.at[i, d - 1],
                near_at[d],
            )
            for d in range(1, n_narrow)
        ]

    for c in range(CHUNKS):
        loads[c].wait()
        value = dot(attended[...], wo[:, cols(c)])
        part[:, cols(c)] = value
        sent_a[:, cols(c)] = value.astype(BF16)
        for copy in scatter(sent_a, got_a, rs_send, rs_recv, c):
            copy.start()
    def spread(c):
        return [
            push(
                ffn_in.at[own, cols(c)],
                ffn_in.at[own, cols(c)],
                ag_send.at[c, d - 1],
                ag_recv.at[c, d - 1],
                near_at[d],
            )
            for d in range(1, n_narrow)
        ]

    scales = [
        push(
            ffn_scale.at[own],
            ffn_scale.at[own],
            sc_send.at[d - 1],
            sc_recv.at[d - 1],
            near_at[d],
        )
        for d in range(1, n_narrow)
    ]
    square = jnp.zeros((mine, 1), F32)
    for c in range(CHUNKS):
        for copy in scatter(sent_a, got_a, rs_send, rs_recv, c):
            copy.wait_recv()
        value = picked[:, cols(c)].astype(F32) + part[own, cols(c)]
        for d in range(n_narrow - 1):
            value = value + got_a[d, :, cols(c)].astype(F32)
        first[:, cols(c)] = value
        ffn_in[own, cols(c)] = (value * ffn_gain[:, cols(c)]).astype(BF16)
        for copy in spread(c):
            copy.start()
        square = square + jnp.sum(value * value, axis=-1, keepdims=True)
    ffn_scale[own, :] = jnp.broadcast_to(lax.rsqrt(square / width + EPS), (mine, LANES))
    for copy in scales:
        copy.start()
    for load in loads[CHUNKS : CHUNKS + 3]:
        load.wait()
    for c in range(CHUNKS):
        for copy in spread(c):
            copy.wait_recv()
        gate_part = dot(ffn_in[:, cols(c)], wg[cols(c), :])
        up_part = dot(ffn_in[:, cols(c)], wu[cols(c), :])
        if c == 0:
            gate_acc[...] = gate_part
            up_acc[...] = up_part
        else:
            gate_acc[...] += gate_part
            up_acc[...] += up_part
    for copy in scales:
        copy.wait_recv()
    row_scale = ffn_scale[:, 0:1]
    gate = gate_acc[...] * row_scale
    hidden = (gate / (1.0 + jnp.exp(-gate)) * (up_acc[...] * row_scale)).astype(BF16)

    upper = w // half
    half_chunks = CHUNKS // 2
    order = [lax.rem((1 - upper) * half_chunks + i, CHUNKS) for i in range(CHUNKS)]
    for i, c in enumerate(order):
        value = dot(hidden, wd[:, cols(c)])
        part[:, cols(c)] = value
        sent_b[:, cols(c)] = value.astype(BF16)
        for copy in scatter(sent_b, got_b, rt_send, rt_recv, i, c):
            copy.start()

    partner_at = {"wide": lax.rem(w + half, n_wide), "narrow": n}

    def swap(i):
        at = pl.ds(i * chunk, chunk)
        return push(
            swap_out.at[:, at], swap_in.at[:, at], swap_send.at[i], swap_recv.at[i], partner_at
        )

    scale_swap = push(
        scale_out, scale_in, swap_send.at[half_chunks], swap_recv.at[half_chunks], partner_at
    )
    square = jnp.zeros((mine, 1), F32)
    for i, c in enumerate(order):
        for copy in scatter(sent_b, got_b, rt_send, rt_recv, i, c):
            copy.wait_recv()
        value = first[:, cols(c)] + part[own, cols(c)]
        for d in range(n_narrow - 1):
            value = value + got_b[d, :, cols(c)].astype(F32)
        if i < half_chunks:
            swap_out[:, pl.ds(i * chunk, chunk)] = value.astype(BF16)
            swap(i).start()
        else:
            first[:, cols(c)] = value
        square = square + jnp.sum(value * value, axis=-1, keepdims=True)
    scale = lax.rsqrt(square / width + EPS)
    scale_out[...] = jnp.broadcast_to(scale, (mine, LANES))
    scale_swap.start()

    def region(source, narrow, i):
        start = lax.rem(source, half) * rows + narrow * mine
        return guided.at[
            pl.ds(pl.multiple_of(start, mine), mine), cols(source // half * half_chunks + i)
        ]

    scale_swap.wait()
    for i in range(half_chunks):
        swap(i).wait()
        c = order[half_chunks + i]
        gain = final_gain[:, cols(c)]
        kept = first[:, cols(c)] * scale * gain
        other = swap_in[:, pl.ds(i * chunk, chunk)].astype(F32) * scale_in[:, 0:1] * gain
        cond = jnp.where(upper == 1, other, kept)
        uncond = jnp.where(upper == 1, kept, other)
        region(w, n, i)[...] = (uncond + GUIDE * (cond - uncond)).astype(BF16)

    parity = lax.rem(w, 2)

    def from_near(d):
        return lax.rem(n + n_narrow - d, n_narrow)

    def near_copy(i, j, d):
        s = place + j
        spot = region(2 * s + parity, n, i)
        return push(spot, spot, n_send.at[i, s, d], n_recv.at[i, s, d], near_at[d])

    def line_copy(route, j, step):
        spot = region(2 * (place + j) + parity, from_near(route % n_narrow), route // n_narrow)
        s = place + j
        way = (step + 1) // 2
        return push(
            spot, spot, l_send.at[route, s, way], l_recv.at[route, s, way], line_at[step]
        )

    def twin_copy(i, j, d):
        spot = region(2 * (place + j) + parity, from_near(d), i)
        s = place + j
        return push(spot, spot, s_send.at[i, s, d], s_recv.at[i, s, d], twin_at)

    def there(j):
        return jnp.logical_and(place + j >= 0, place + j < pairs)

    def line_go(route, j, act):
        for step in (1, -1):
            if j * step <= 0:
                pl.when(jnp.logical_and(there(j), there(step)))(
                    lambda step=step: act(line_copy(route, j, step))
                )

    def line_take(route, j):
        line_copy(route, j, -1 if j > 0 else 1).wait_recv()

    def start(copy):
        copy.start()

    def all_near(j, act):
        for d in range(1, n_narrow):
            act(near_copy(0, j, d))

    routes = [0] + [n_narrow + d for d in range(n_narrow)]
    line_go(0, 0, start)
    for d in range(1, n_narrow):
        near_copy(1, 0, d).start()
    line_go(n_narrow, 0, start)
    all_near(0, start)
    twin_copy(0, 0, 0).start()
    twin_copy(1, 0, 0).start()
    for d in range(1, n_narrow):
        near_copy(1, 0, d).wait_recv()
        line_go(n_narrow + d, 0, start)
        twin_copy(1, 0, d).start()

    def near_take(j):
        for d in range(1, n_narrow):
            near_copy(0, j, d).wait_recv()
            twin_copy(0, j, d).start()

    near_take(0)
    for reach in range(1, pairs):
        for j in (-reach, reach):

            def arrive(j=j):
                line_take(0, j)
                line_go(0, j, start)
                all_near(j, start)
                twin_copy(0, j, 0).start()
                for d in range(n_narrow):
                    line_take(n_narrow + d, j)
                    line_go(n_narrow + d, j, start)
                    twin_copy(1, j, d).start()

            pl.when(there(j))(arrive)
        for j in (-reach, reach):
            pl.when(there(j))(functools.partial(near_take, j))
    for i in range(half_chunks):
        for s in range(pairs):
            for d in range(n_narrow):
                twin_copy(i, s - place, d).wait_recv()

    loads[CHUNKS + 3].wait()
    tile = 256

    def logit_tile(j, carry):
        at = pl.ds(pl.multiple_of(j * tile, tile), tile)
        logits[:, at] = dot(guided[...], wh[:, at])
        return carry

    lax.fori_loop(0, logits.shape[1] // tile, logit_tile, 0)
    step = 64

    def row_stats(i, carry):
        at = pl.ds(pl.multiple_of(i * step, step), step)
        value = logits[at, :]
        top = jnp.max(value, axis=-1, keepdims=True)
        total = jnp.sum(jnp.exp(value - top), axis=-1, keepdims=True)
        row_peak[at, :] = jnp.broadcast_to(top, (step, row_peak.shape[1]))
        row_total[at, :] = jnp.broadcast_to(total, (step, row_peak.shape[1]))
        return carry

    count = logits.shape[0]
    lax.fori_loop(0, count // step, row_stats, 0)
    peak = row_peak[...].T[0:1, :]
    total = row_total[...].T[0:1, :]

    slot = 0
    for stage, places in enumerate(([twin_at] + near_at[1:] + cross_at, far_at[1:])):
        board[slot, :, 0:count] = peak
        board[slot, :, count:] = total
        copies = [
            push(
                board.at[slot],
                board.at[slot + 1 + i],
                st_send.at[slot + 1 + i],
                st_recv.at[slot + 1 + i],
                where,
            )
            for i, where in enumerate(places)
        ]
        for copy in copies:
            copy.start()
        for copy in copies:
            copy.wait()
        top = peak
        for i in range(len(places)):
            top = jnp.maximum(top, board[slot + 1 + i, :, 0:count])
        total = total * jnp.exp(peak - top)
        for i in range(len(places)):
            got = board[slot + 1 + i]
            total = total + got[:, count:] * jnp.exp(got[:, 0:count] - top)
        peak = top
        slot += 1 + len(places)
    stats[0:1, :] = peak + jnp.log(total)
    stats[1:2, :] = 1.0 / total

    for copy in scales:
        copy.wait_send()
    for i, c in enumerate(order):
        for copy in scatter(sent_a, got_a, rs_send, rs_recv, i):
            copy.wait_send()
        for copy in scatter(sent_b, got_b, rt_send, rt_recv, i, c):
            copy.wait_send()
        for copy in spread(i):
            copy.wait_send()

    def sent(copy):
        copy.wait_send()

    for d in range(1, n_narrow):
        near_copy(1, 0, d).wait_send()
    for i in range(half_chunks):
        for s in range(pairs):
            for d in range(n_narrow):
                twin_copy(i, s - place, d).wait_send()
    for s in range(pairs):
        all_near(s - place, sent)
    for j in range(1 - pairs, pairs):
        for route in routes:
            line_go(route, j, sent)


def tail(n_wide, n_narrow, attended, picked, ffn_gain, final_gain, *weights):
    w_out, w_gate, w_up, w_down, w_head = weights
    rows = attended.shape[0]
    width = picked.shape[1]
    mine = rows // n_narrow
    pairs = n_wide // 2
    total_rows = rows * pairs
    vocab_cols = w_head.shape[1]
    vmem = pl.BlockSpec(memory_space=pltpu.VMEM)
    hbm = pl.BlockSpec(memory_space=pl.ANY)
    near = n_narrow - 1
    slots = 2 + 1 + 2 * near + pairs - 1
    dma = pltpu.SemaphoreType.DMA
    return pl.pallas_call(
        functools.partial(tail_kernel, n_wide, n_narrow),
        out_shape=(
            jax.ShapeDtypeStruct((total_rows, vocab_cols), F32),
            jax.ShapeDtypeStruct((2, total_rows), F32),
        ),
        in_specs=[vmem] * 4 + [hbm] * 5,
        out_specs=(vmem, vmem),
        scratch_shapes=[pltpu.VMEM(v.shape, BF16) for v in weights]
        + [
            pltpu.VMEM((rows, width), F32),
            pltpu.VMEM((rows, width), BF16),
            pltpu.VMEM((rows, width), BF16),
            pltpu.VMEM((near, mine, width), BF16),
            pltpu.VMEM((near, mine, width), BF16),
            pltpu.VMEM((mine, width), F32),
            pltpu.VMEM((rows, width), BF16),
            pltpu.VMEM((rows, w_gate.shape[1]), F32),
            pltpu.VMEM((rows, w_gate.shape[1]), F32),
            pltpu.VMEM((mine, width // 2), BF16),
            pltpu.VMEM((mine, width // 2), BF16),
            pltpu.VMEM((rows, LANES), F32),
            pltpu.VMEM((mine, LANES), F32),
            pltpu.VMEM((mine, LANES), F32),
            pltpu.VMEM((total_rows, width), BF16),
            pltpu.VMEM((total_rows, 128), F32),
            pltpu.VMEM((total_rows, 128), F32),
            pltpu.VMEM((slots, 1, 2 * total_rows), F32),
            dma((CHUNKS + 4,)),
            dma((CHUNKS, near)),
            dma((CHUNKS, near)),
            dma((CHUNKS, near)),
            dma((CHUNKS, near)),
            dma((CHUNKS, near)),
            dma((CHUNKS, near)),
            dma((CHUNKS // 2 + 1,)),
            dma((CHUNKS // 2 + 1,)),
            dma((near,)),
            dma((near,)),
            dma((2 * n_narrow, pairs, 2)),
            dma((2 * n_narrow, pairs, 2)),
            dma((2, pairs, n_narrow)),
            dma((2, pairs, n_narrow)),
            dma((2, pairs, n_narrow)),
            dma((2, pairs, n_narrow)),
            dma((slots,)),
            dma((slots,)),
        ],
        compiler_params=pltpu.CompilerParams(
            collective_id=1, has_side_effects=True, vmem_limit_bytes=60 * 2**20
        ),
    )(attended, picked, ffn_gain, final_gain, *weights)


def on_device(
    block_states,
    attn_gain,
    ffn_gain,
    final_gain,
    w_query,
    w_keyval,
    w_out,
    w_gate,
    w_up,
    w_down,
    w_head,
    cache,
    prefix_lengths,
    masked_positions,
):
    n_wide = lax.axis_size("wide")
    n_narrow = lax.axis_size("narrow")
    wide_index = lax.axis_index("wide")
    narrow_index = lax.axis_index("narrow")
    half_wide = n_wide // 2
    local_req, block, _ = block_states.shape
    masked = masked_positions.shape[1]
    width = w_query.shape[0]

    full_rows, normed = gather_rows(
        n_narrow, block_states.reshape(local_req * block, -1), attn_gain[None, :]
    )
    full_rows = full_rows.reshape(local_req, block, width)

    kv_head = narrow_index // (n_narrow // KVH)
    head_weight = lax.dynamic_slice_in_dim(w_keyval, kv_head * (2 * HD), 2 * HD, 1)
    block_kv = dot(normed, head_weight).astype(BF16).reshape(local_req, block, 2 * HD)
    cache_kv = lax.dynamic_index_in_dim(cache, kv_head, axis=2, keepdims=False)
    first_req = wide_index % half_wide * local_req
    my_positions = lax.dynamic_slice_in_dim(masked_positions, first_req, local_req, 0)
    choose = (my_positions[:, :, None] == jnp.arange(block)[None, None, :]).astype(BF16)
    picked = jnp.einsum("bml,bld->bmd", choose, full_rows, preferred_element_type=F32)
    picked = picked.astype(BF16).reshape(local_req * masked, width)
    mine = local_req * masked // n_narrow
    picked = lax.dynamic_slice_in_dim(picked, narrow_index * mine, mine, 0)
    local_heads = w_query.shape[1] // HD
    query = dot(normed, w_query).astype(BF16).reshape(local_req, block, local_heads * HD)
    query = jnp.einsum("bml,bld->bmd", choose, query, preferred_element_type=F32).astype(BF16)
    query = query.reshape(local_req, masked, local_heads, HD)
    scale = 1.0 / math.sqrt(HD)
    pre_scores = (
        jnp.einsum("bmhd,bpd->bhmp", query, cache_kv[..., :HD], preferred_element_type=F32) * scale
    )
    live = jnp.arange(cache_kv.shape[1])[None, :] < prefix_lengths[:, None]
    pre_scores = jnp.where(live[:, None, None, :], pre_scores, -jnp.inf)
    blk_scores = (
        jnp.einsum("bmhd,bld->bhml", query, block_kv[..., :HD], preferred_element_type=F32) * scale
    )
    peak = jnp.maximum(
        jnp.max(pre_scores, axis=-1, keepdims=True), jnp.max(blk_scores, axis=-1, keepdims=True)
    )
    pre_weights = jnp.exp(pre_scores - peak)
    blk_weights = jnp.exp(blk_scores - peak)
    weight_total = jnp.sum(pre_weights, axis=-1, keepdims=True) + jnp.sum(
        blk_weights, axis=-1, keepdims=True
    )
    pre_probs = (pre_weights / weight_total).astype(BF16)
    blk_probs = (blk_weights / weight_total).astype(BF16)
    attended = jnp.einsum(
        "bhmp,bpd->bmhd", pre_probs, cache_kv[..., HD:], preferred_element_type=F32
    )
    attended = attended + jnp.einsum(
        "bhml,bld->bmhd", blk_probs, block_kv[..., HD:], preferred_element_type=F32
    )
    attended = attended.astype(BF16).reshape(local_req * masked, local_heads * HD)

    logits, stats = tail(
        n_wide,
        n_narrow,
        attended,
        picked,
        ffn_gain[None, :],
        final_gain[None, :],
        w_out,
        w_gate,
        w_up,
        w_down,
        w_head,
    )
    return logits - stats[0][:, None], stats[1].reshape(-1, masked)


def solution(mesh):
    in_specs = (
        P("wide", None, "narrow"),
        P(),
        P(),
        P(),
        P(None, "narrow"),
        P(),
        P("narrow", None),
        P(None, "narrow"),
        P(None, "narrow"),
        P("narrow", None),
        P(None, ("wide", "narrow")),
        P("wide", None, None, None),
        P("wide"),
        P(),
    )
    out_specs = (P(None, ("wide", "narrow")), P())
    return jax.shard_map(
        on_device, mesh=mesh, in_specs=in_specs, out_specs=out_specs, check_vma=False
    )
```
